32 devices in a mesh: row: 8 (over z, y), col: 4 (over x, core).
Axes of the slice: x: 2, y: 2, z: 4, core: 2. Of those that a mesh axis runs over, the one named last changes fastest.
Arguments:
- object_field: float32 [2, 3, 2048, 1024], P(None, None, 'row', 'col'), may hold values from -1 to 1
- probe: float32 [2, 128, 128], replicated, may hold values from -4 to 4
- propagator: float32 [128, 128], replicated, may hold values from -3.140625 to 3.140625
- measured: float32 [8, 4, 6, 128, 128], P('row', 'col'), may hold values from 0 to 1
- offsets: int32 [8, 4, 6, 2], P('row', 'col'), may hold values from 0 to 255
Outputs:
- updated: float32 [2, 3, 2048, 1024], P(None, None, 'row', 'col')
The draws below stay inside these ranges and needn't reach their ends.
Inputs may be any that keep to these rules, and one draw needn't show every extreme that they name: `offsets`: entry 0 is the row offset and entry 1 the column offset of a window inside its tile.
All inputs are finite; a program needn't handle non-finite values.
Results may differ from the reference program's by a relative error of at most 0.0003.
Values sent between devices are 32-bit elements; how exact they have to be, the bound alone decides.
A program may use at most 64 MiB of HBM per device.

```python
import jax
import jax.numpy as jnp
from jax import lax

PROBE = 128
SLICES = 3
POS = 6
ITERS = 2
TILE = 256
ROWS_ALL = 2048
COLS_ALL = 1024
N_ROW = 8
N_COL = 4


def with_ends(drawn, own_key, least, largest):
    extent = drawn.shape
    index_at = [jax.random.randint(jax.random.fold_in(own_key, axis), (), 0, extent[axis]) for axis in range(len(extent))]
    drawn = drawn.at[tuple(index_at)].set(least)
    longest = extent.index(max(extent))
    index_at[longest] = (index_at[longest] + 1) % extent[longest]
    return drawn.at[tuple(index_at)].set(largest)


def levels(stream_key, dims, shards, least, high):
    gain, own = 1.0, jax.random.fold_in(stream_key, 6)
    for position, parts in shards:
        draws = jnp.exp(jax.random.uniform(jax.random.fold_in(own, position), (parts,), jnp.float32, least / len(shards), high / len(shards)))
        gain = gain * jnp.repeat(draws, dims[position] // parts).reshape([-1 if axis == position else 1 for axis in range(len(dims))])
    return gain


def noise(key, extent, deviation, limit, held_as=jnp.bfloat16):
    array = deviation * jax.random.normal(key, extent, jnp.float32)
    return jnp.clip(array, min=-limit, max=limit).astype(held_as)


def setup_inputs(seed: int = 0) -> dict:
    key_of = jax.random.split(jax.random.key(seed), 6)
    object_field = jnp.clip(jax.random.uniform(key_of[0], (2, SLICES, ROWS_ALL, COLS_ALL), jnp.float32, -1.0, 1.0) * levels(key_of[0], (2, SLICES, ROWS_ALL, COLS_ALL), ((2, 8), (3, 4)), -0.4, 0.0), -1.0, 1.0)
    probe = noise(key_of[1], (2, PROBE, PROBE), 1.0, 4.0, jnp.float32)
    propagator = jnp.clip(jax.random.uniform(key_of[2], (PROBE, PROBE), jnp.float32, -3.140625, 3.140625), -3.140625, 3.140625)
    measured = jnp.clip(1.0 * jax.random.uniform(key_of[3], (N_ROW, N_COL, POS, PROBE, PROBE), jnp.float32) ** levels(key_of[3], (N_ROW, N_COL, POS, PROBE, PROBE), ((0, 8), (1, 4)), -0.2, 0.2), 0.0, 1.0)
    offsets = with_ends(jax.random.randint(key_of[4], (N_ROW, N_COL, POS, 2), 0, TILE), jax.random.fold_in(key_of[4], 1), 0, TILE - 1).astype(jnp.int32)
    return {"object_field": object_field, "probe": probe, "propagator": propagator, "measured": measured, "offsets": offsets}


step_size = 0.05

def total_loss(field, probe, propagator, measured, offsets):
    wrapped = jnp.concatenate([field, field[:, :, :PROBE, :]], axis=2)
    wrapped = jnp.concatenate([wrapped, wrapped[:, :, :, :PROBE]], axis=3)
    row_base = (jnp.arange(N_ROW, dtype=jnp.int32) * TILE)[:, None, None] + offsets[:, :, :, 0].astype(jnp.int32)
    col_base = (jnp.arange(N_COL, dtype=jnp.int32) * TILE)[None, :, None] + offsets[:, :, :, 1].astype(jnp.int32)
    initial = probe[0] + 1j * probe[1]
    transfer = jnp.exp(1j * propagator)

    def one_position(start_row, start_col, target):
        anchor = jnp.zeros((), jnp.int32)
        patch = lax.dynamic_slice(wrapped, (anchor, anchor, start_row, start_col), (2, SLICES, PROBE, PROBE))
        wave = initial
        for layer in range(SLICES):
            wave = wave * (patch[0, layer] + 1j * patch[1, layer])
            if layer + 1 < SLICES:
                wave = jnp.fft.ifft2(jnp.fft.fft2(wave, norm='ortho') * transfer, norm='ortho')
        far = jnp.fft.fft2(wave, norm='ortho')
        power = jnp.real(far) ** 2 + jnp.imag(far) ** 2
        return jnp.sum((power - target) ** 2)

    def one_row(inputs):
        rows_here, cols_here, targets = inputs
        values = jax.vmap(one_position)(rows_here.reshape(-1), cols_here.reshape(-1), targets.reshape(-1, PROBE, PROBE))
        return jnp.sum(values)
    return jnp.sum(lax.map(one_row, (row_base, col_base, measured)))

def reference(object_field, probe, propagator, measured, offsets):
    field = object_field
    for step in range(ITERS):
        field = field - step_size * jax.grad(total_loss)(field, probe, propagator, measured, offsets)
    return field
```

```python
import jax
import jax.numpy as jnp
import numpy as np
from jax import lax
from jax.experimental import pallas as pl
from jax.experimental.pallas import tpu as pltpu
from jax.sharding import PartitionSpec as P

ITERS = 2
STEP = 0.05
SUB = 8
F32, BF16 = jnp.float32, jnp.bfloat16


def passed_along(block, axis, distance):
    n = lax.axis_size(axis)
    return lax.ppermute(block, axis, [((i - distance) % n, i) for i in range(n)])


def tables(h):
    k = np.arange(h)
    angle = (k[:, None] * k[None, :] % h) * (-2.0 * np.pi / h)
    c, s = np.cos(angle) / np.sqrt(h), np.sin(angle) / np.sqrt(h)

    def halves(m):
        m = m.astype(np.float32)
        high = m.astype(jnp.bfloat16)
        return high, (m - high.astype(np.float32)).astype(jnp.bfloat16)

    ah, al = halves(np.block([[c, s], [-s, c]]))
    bh, bl = halves(np.block([[c, -s], [s, c]]))
    right = [np.concatenate([x, x, y], 0) for x, y in ((ah, al), (bh, bl))]
    left = [np.concatenate([x, x, y], 1) for x, y in ((bh, bl), (ah, al))]
    return np.stack(right), np.stack(left)


def split(x):
    high = x.astype(BF16)
    return high, (x - high.astype(F32)).astype(BF16)


def mul_right(x, table):
    high, low = split(x)
    return jnp.dot(jnp.concatenate([high, low, high], 1), table, preferred_element_type=F32)


def mul_left(x, table):
    high, low = split(x)
    return jnp.dot(table, jnp.concatenate([high, low, high], 0), preferred_element_type=F32)


def to_left(x, h, n):
    return jnp.concatenate(
        [jnp.concatenate([x[p * h:(p + 1) * h, k * h:(k + 1) * h] for p in range(n)], 1) for k in range(2)], 0)


def to_right(x, h, n):
    return jnp.concatenate(
        [jnp.concatenate([x[k * h:(k + 1) * h, p * h:(p + 1) * h] for k in range(2)], 1) for p in range(n)], 0)


def dft(x, tab, h, n):
    return mul_left(to_left(mul_right(x, tab[0][0]), h, n), tab[1][0])


def idft(x, tab, h, n):
    return mul_right(to_right(mul_left(x, tab[1][1]), h, n), tab[0][1])


def propagate(x, tab, phase, sign, h, n):
    y = dft(x, tab, h, n)
    cr, ci = phase[0], phase[1] * sign
    cr, ci = (jnp.concatenate([v] * n, 1) for v in (cr, ci))
    a, b = y[:h], y[h:]
    return idft(jnp.concatenate([a * cr - b * ci, a * ci + b * cr], 0), tab, h, n)


def times(x, o, sign, h):
    a, b, c, d = x[:, :h], x[:, h:], o[:, :h], o[:, h:]
    if sign < 0:
        return jnp.concatenate([a * c + b * d, b * c - a * d], 1)
    return jnp.concatenate([a * c - b * d, a * d + b * c], 1)


def gather(ext, r, c, h):
    lane = lax.broadcasted_iota(jnp.int32, (h + SUB, h), 1)
    sub = lax.broadcasted_iota(jnp.int32, (h // SUB, SUB, h), 1)
    q, m, t = c // h, c % h, r % SUB
    parts = []
    for k in range(2):
        lines = ext[k, pl.ds(pl.multiple_of(r - t, SUB), h + SUB), pl.ds(pl.multiple_of(q * h, h), 2 * h)]
        mixed = jnp.where(lane >= m, lines[:, :h], lines[:, h:])
        mixed = pltpu.roll(mixed, (h - m) % h, 1).reshape(h // SUB + 1, SUB, h)
        mixed = jnp.where(sub >= t, mixed[:-1], mixed[1:])
        parts.append(pltpu.roll(mixed, (SUB - t) % SUB, 1).reshape(h, h))
    return jnp.concatenate(parts, 1)


def scatter(acc, g, r, c, h):
    lane = lax.broadcasted_iota(jnp.int32, (h + SUB, h), 1)
    sub = lax.broadcasted_iota(jnp.int32, (h // SUB + 1, SUB, h), 1)
    q, m, t = c // h, c % h, r % SUB
    empty = jnp.zeros((1, SUB, h), F32)
    for k in range(2):
        rolled = pltpu.roll(g[:, k * h:(k + 1) * h].reshape(h // SUB, SUB, h), t, 1)
        rolled = jnp.where(sub >= t, jnp.concatenate([rolled, empty], 0), jnp.concatenate([empty, rolled], 0))
        rolled = pltpu.roll(rolled.reshape(h + SUB, h), m, 1)
        keep = lane >= m
        pair = jnp.concatenate([jnp.where(keep, rolled, 0.0), jnp.where(keep, 0.0, rolled)], 1)
        at = (k, pl.ds(pl.multiple_of(r - t, SUB), h + SUB), pl.ds(pl.multiple_of(q * h, h), 2 * h))
        acc[at] = acc[at] + pair


def groups(n):
    size = 2 if n % 2 == 0 else 1
    return [list(range(i, i + size)) for i in range(0, n, size)]


def fill(ext, tall, right):
    w = tall.shape[2]
    ext[:, :, :w] = tall[...]
    ext[:, :, w:] = right[...]


def read_windows(ext, offs, ps, h):
    return jnp.concatenate([gather(ext, offs[p, 0], offs[p, 1], h) for p in ps], 0)


def tiled_probe(probe, n):
    one = jnp.concatenate([probe[0], probe[1]], 1)
    return jnp.concatenate([one] * n, 0)


def tab_of(tr, tl):
    return ([tr[0], tr[1]], [tl[0], tl[1]])


def rows_of(ps, h):
    return slice(ps[0] * h, (ps[-1] + 1) * h)


def k_first(offs, tall, right, probe, phase, tr, tl, w_out, ext):
    h, tab = probe.shape[1], tab_of(tr, tl)
    fill(ext, tall, right)
    for ps in groups(offs.shape[0]):
        n = len(ps)
        x = times(tiled_probe(probe, n), read_windows(ext, offs, ps, h), 1, h)
        w_out[rows_of(ps, h)] = propagate(x, tab, phase, 1.0, h, n)


def k_second(offs, tall, right, w_in, phase, tr, tl, w_out, o_out, ext):
    h, tab = phase.shape[1], tab_of(tr, tl)
    fill(ext, tall, right)
    for ps in groups(offs.shape[0]):
        n, rows = len(ps), rows_of(ps, h)
        o = read_windows(ext, offs, ps, h)
        o_out[rows] = o
        w_out[rows] = propagate(times(w_in[rows], o, 1, h), tab, phase, 1.0, h, n)


def emit(acc, gl, gr):
    w = gl.shape[2]
    gl[...] = acc[:, :, :w]
    gr[...] = acc[:, :, w:]


def k_last(offs, tall, right, w_in, measured, tr, tl, gl, gr, g_out, ext, acc):
    h, tab = measured.shape[1], tab_of(tr, tl)
    fill(ext, tall, right)
    acc[...] = jnp.zeros_like(acc)
    for ps in groups(offs.shape[0]):
        n, rows = len(ps), rows_of(ps, h)
        o = read_windows(ext, offs, ps, h)
        w = w_in[rows]
        far = dft(times(w, o, 1, h), tab, h, n)
        a, b = far[:h], far[h:]
        target = jnp.concatenate([measured[p] for p in ps], 1)
        f = 4.0 * (a * a + b * b - target)
        g = idft(jnp.concatenate([a * f, b * f], 0), tab, h, n)
        go = times(g, w, -1, h)
        g_out[rows] = times(g, o, -1, h)
        for i, p in enumerate(ps):
            scatter(acc, go[i * h:(i + 1) * h], offs[p, 0], offs[p, 1], h)
    emit(acc, gl, gr)


def k_back(offs, g_in, w_in, o_in, phase, tr, tl, gl, gr, g_out, acc):
    h, tab = phase.shape[1], tab_of(tr, tl)
    acc[...] = jnp.zeros_like(acc)
    for ps in groups(offs.shape[0]):
        n, rows = len(ps), rows_of(ps, h)
        g = propagate(g_in[rows], tab, phase, -1.0, h, n)
        go = times(g, w_in[rows], -1, h)
        g_out[rows] = times(g, o_in[rows], -1, h)
        for i, p in enumerate(ps):
            scatter(acc, go[i * h:(i + 1) * h], offs[p, 0], offs[p, 1], h)
    emit(acc, gl, gr)


def k_back_first(offs, g_in, probe, phase, tr, tl, gl, gr, acc):
    h, tab = phase.shape[1], tab_of(tr, tl)
    acc[...] = jnp.zeros_like(acc)
    for ps in groups(offs.shape[0]):
        n, rows = len(ps), rows_of(ps, h)
        g = propagate(g_in[rows], tab, phase, -1.0, h, n)
        go = times(g, tiled_probe(probe, n), -1, h)
        for i, p in enumerate(ps):
            scatter(acc, go[i * h:(i + 1) * h], offs[p, 0], offs[p, 1], h)
    emit(acc, gl, gr)


def on_device(object_field, probe, propagator, measured, offsets):
    slices, tile_r, tile_c = object_field.shape[1:]
    h, pos = probe.shape[1], offsets.shape[2]
    offs = offsets.reshape(pos, 2)
    target = measured.reshape(pos, h, h)
    phase = jnp.stack([jnp.cos(propagator), jnp.sin(propagator)])
    tr, tl = (jnp.asarray(t) for t in tables(h))

    wave = jax.ShapeDtypeStruct((pos * h, 2 * h), F32)
    ext = pltpu.VMEM((2, tile_r + h, tile_c + h), F32)
    grad = [jax.ShapeDtypeStruct((2, tile_r + h, tile_c), F32), jax.ShapeDtypeStruct((2, tile_r + h, h), F32)]
    flops = 2 * 2 * 2 * 3 * pos * h * (2 * h) ** 2
    cost = pl.CostEstimate(flops=flops, bytes_accessed=6_000_000, transcendentals=0)

    def call(body, outs, scratch, *args):
        vmem = pl.BlockSpec(memory_space=pltpu.VMEM)
        return pl.pallas_call(
            body,
            out_shape=outs,
            in_specs=[pl.BlockSpec(memory_space=pltpu.SMEM)] + [vmem] * len(args),
            out_specs=[vmem] * len(outs),
            scratch_shapes=scratch,
            cost_estimate=cost,
            compiler_params=pltpu.CompilerParams(vmem_limit_bytes=40 * 1024 * 1024),
        )(offs, *args)

    tall, right = [], []
    for s in range(slices):
        own = object_field[:, s]
        tall.append(jnp.concatenate([own, passed_along(own[:, :h], "row", -1)], 1))
    for s in range(slices):
        right.append(passed_along(tall[s][:, :, :h], "col", -1))

    result = [None] * slices
    for step in range(ITERS):
        waves, objects = [None], [None]
        (w,) = call(k_first, [wave], [ext], tall[0], right[0], probe, phase, tr, tl)
        waves.append(w)
        for s in range(1, slices - 1):
            w, o = call(k_second, [wave, wave], [ext], tall[s], right[s], waves[s], phase, tr, tl)
            waves.append(w)
            objects.append(o)
        s = slices - 1
        grads = [None] * slices
        *grads[s], g = call(k_last, grad + [wave], [ext, ext], tall[s], right[s], waves[s], target, tr, tl)
        for s in range(slices - 2, 0, -1):
            *grads[s], g = call(k_back, grad + [wave], [ext], g, waves[s], objects[s], phase, tr, tl)
        grads[0] = call(k_back_first, grad, [ext], g, probe, phase, tr, tl)
        last = step + 1 == ITERS
        for s in range(slices - 1, -1, -1):
            gl, gr = grads[s]
            total = gl.at[:, :, :h].add(passed_along(gr, "col", 1))
            above = passed_along(total[:, tile_r:], "row", 1)
            if last:
                result[s] = tall[s][:, :tile_r] - STEP * total[:, :tile_r].at[:, :h].add(above)
            else:
                below = passed_along(total[:, :h], "row", -1)
                total = total.at[:, :h].add(above).at[:, tile_r:].add(below)
                tall[s] = tall[s] - STEP * total
                right[s] = passed_along(tall[s][:, :, :h], "col", -1)
    return jnp.stack(result, 1)


def solution(mesh):
    return jax.shard_map(
        on_device,
        mesh=mesh,
        in_specs=(
            P(None, None, "row", "col"),
            P(),
            P(),
            P("row", "col", None, None, None),
            P("row", "col", None, None),
        ),
        out_specs=P(None, None, "row", "col"),
        check_vma=False,
    )
```

```python
import jax
import jax.numpy as jnp
import numpy as np
from jax import lax
from jax.experimental import pallas as pl
from jax.experimental.pallas import tpu as pltpu
from jax.sharding import PartitionSpec as P

ITERS = 2
STEP = 0.05
SUB = 8
F32, BF16 = jnp.float32, jnp.bfloat16


def passed_along(block, axis, distance):
    n = lax.axis_size(axis)
    return lax.ppermute(block, axis, [((i - distance) % n, i) for i in range(n)])


def after(value, *others):
    return lax.optimization_barrier((value, *others))[0] if others else value


def tables(h):
    k = np.arange(h)
    angle = (k[:, None] * k[None, :] % h) * (-2.0 * np.pi / h)
    c, s = np.cos(angle) / np.sqrt(h), np.sin(angle) / np.sqrt(h)

    def halves(m):
        m = m.astype(np.float32)
        high = m.astype(jnp.bfloat16)
        return high, (m - high.astype(np.float32)).astype(jnp.bfloat16)

    ah, al = halves(np.block([[c, s], [-s, c]]))
    bh, bl = halves(np.block([[c, -s], [s, c]]))
    return np.stack([ah, bh]), np.stack([al, bl])


def split(x):
    high = x.astype(BF16)
    return high, (x - high.astype(F32)).astype(BF16)


def mul_right(x, table):
    high, low = split(x)
    return jnp.dot(jnp.concatenate([high, low, high], 1), table, preferred_element_type=F32)


def mul_left(x, table):
    high, low = split(x)
    return jnp.dot(table, jnp.concatenate([high, low, high], 0), preferred_element_type=F32)


def to_left(x, h, n):
    return jnp.concatenate(
        [jnp.concatenate([x[p * h:(p + 1) * h, k * h:(k + 1) * h] for p in range(n)], 1) for k in range(2)], 0)


def to_right(x, h, n):
    return jnp.concatenate(
        [jnp.concatenate([x[k * h:(k + 1) * h, p * h:(p + 1) * h] for k in range(2)], 1) for p in range(n)], 0)


def dft(x, tab, h, n):
    return mul_left(to_left(mul_right(x, tab[0][0]), h, n), tab[1][0])


def idft(x, tab, h, n):
    return mul_right(to_right(mul_left(x, tab[1][1]), h, n), tab[0][1])


def propagate(x, tab, phase, sign, h, n):
    y = dft(x, tab, h, n)
    cr, ci = phase[0], phase[1] * sign
    cr, ci = (jnp.concatenate([v] * n, 1) for v in (cr, ci))
    a, b = y[:h], y[h:]
    return idft(jnp.concatenate([a * cr - b * ci, a * ci + b * cr], 0), tab, h, n)


def times(x, o, sign, h):
    a, b, c, d = x[:, :h], x[:, h:], o[:, :h], o[:, h:]
    if sign < 0:
        return jnp.concatenate([a * c + b * d, b * c - a * d], 1)
    return jnp.concatenate([a * c - b * d, a * d + b * c], 1)


def gather(ext, r, c, h):
    lane = lax.broadcasted_iota(jnp.int32, (h + SUB, h), 1)
    sub = lax.broadcasted_iota(jnp.int32, (h // SUB, SUB, h), 1)
    q, m, t = c // h, c % h, r % SUB
    parts = []
    for k in range(2):
        lines = ext[k, pl.ds(pl.multiple_of(r - t, SUB), h + SUB), pl.ds(pl.multiple_of(q * h, h), 2 * h)]
        mixed = jnp.where(lane >= m, lines[:, :h], lines[:, h:])
        mixed = pltpu.roll(mixed, (h - m) % h, 1).reshape(h // SUB + 1, SUB, h)
        mixed = jnp.where(sub >= t, mixed[:-1], mixed[1:])
        parts.append(pltpu.roll(mixed, (SUB - t) % SUB, 1).reshape(h, h))
    return jnp.concatenate(parts, 1)


def scatter(acc, g, r, c, h):
    lane = lax.broadcasted_iota(jnp.int32, (h + SUB, h), 1)
    sub = lax.broadcasted_iota(jnp.int32, (h // SUB + 1, SUB, h), 1)
    q, m, t = c // h, c % h, r % SUB
    empty = jnp.zeros((1, SUB, h), F32)
    for k in range(2):
        rolled = pltpu.roll(g[:, k * h:(k + 1) * h].reshape(h // SUB, SUB, h), t, 1)
        rolled = jnp.where(sub >= t, jnp.concatenate([rolled, empty], 0), jnp.concatenate([empty, rolled], 0))
        rolled = pltpu.roll(rolled.reshape(h + SUB, h), m, 1)
        keep = lane >= m
        pair = jnp.concatenate([jnp.where(keep, rolled, 0.0), jnp.where(keep, 0.0, rolled)], 1)
        at = (k, pl.ds(pl.multiple_of(r - t, SUB), h + SUB), pl.ds(pl.multiple_of(q * h, h), 2 * h))
        acc[at] = acc[at] + pair


def groups(n):
    size = 2 if n % 2 == 0 else 1
    return [list(range(i, i + size)) for i in range(0, n, size)]


def fill(ext, tall, right):
    w = tall.shape[2]
    ext[:, :, :w] = tall[...]
    ext[:, :, w:] = right[...]


def read_windows(ext, offs, ps, h):
    return jnp.concatenate([gather(ext, offs[p, 0], offs[p, 1], h) for p in ps], 0)


def tiled_probe(probe, n):
    one = jnp.concatenate([probe[0], probe[1]], 1)
    return jnp.concatenate([one] * n, 0)


def tab_of(tr, tl):
    pairs = [(tr[i], tl[i]) for i in range(2)]
    return ([jnp.concatenate([x, x, y], 0) for x, y in pairs], [jnp.concatenate([x, x, y], 1) for x, y in pairs[::-1]])


def rows_of(ps, h):
    return slice(ps[0] * h, (ps[-1] + 1) * h)


def k_first(offs, tall, right, probe, phase, tr, tl, w_out, ext):
    h, tab = probe.shape[1], tab_of(tr, tl)
    fill(ext, tall, right)
    for ps in groups(offs.shape[0]):
        n = len(ps)
        x = times(tiled_probe(probe, n), read_windows(ext, offs, ps, h), 1, h)
        w_out[rows_of(ps, h)] = propagate(x, tab, phase, 1.0, h, n)


def k_second(offs, tall, right, w_in, phase, tr, tl, w_out, o_out, ext):
    h, tab = phase.shape[1], tab_of(tr, tl)
    fill(ext, tall, right)
    for ps in groups(offs.shape[0]):
        n, rows = len(ps), rows_of(ps, h)
        o = read_windows(ext, offs, ps, h)
        o_out[rows] = o
        w_out[rows] = propagate(times(w_in[rows], o, 1, h), tab, phase, 1.0, h, n)


def emit(acc, gl, gr):
    w = gl.shape[2]
    gl[...] = acc[:, :, :w]
    gr[...] = acc[:, :, w:]


def k_last(offs, tall, right, w_in, measured, tr, tl, gl, gr, g_out, ext, acc):
    h, tab = measured.shape[1], tab_of(tr, tl)
    fill(ext, tall, right)
    acc[...] = jnp.zeros_like(acc)
    for ps in groups(offs.shape[0]):
        n, rows = len(ps), rows_of(ps, h)
        o = read_windows(ext, offs, ps, h)
        w = w_in[rows]
        far = dft(times(w, o, 1, h), tab, h, n)
        a, b = far[:h], far[h:]
        target = jnp.concatenate([measured[p] for p in ps], 1)
        f = 4.0 * (a * a + b * b - target)
        g = idft(jnp.concatenate([a * f, b * f], 0), tab, h, n)
        go = times(g, w, -1, h)
        g_out[rows] = times(g, o, -1, h)
        for i, p in enumerate(ps):
            scatter(acc, go[i * h:(i + 1) * h], offs[p, 0], offs[p, 1], h)
    emit(acc, gl, gr)


def k_back(offs, g_in, w_in, o_in, phase, tr, tl, gl, gr, g_out, acc):
    h, tab = phase.shape[1], tab_of(tr, tl)
    acc[...] = jnp.zeros_like(acc)
    for ps in groups(offs.shape[0]):
        n, rows = len(ps), rows_of(ps, h)
        g = propagate(g_in[rows], tab, phase, -1.0, h, n)
        go = times(g, w_in[rows], -1, h)
        g_out[rows] = times(g, o_in[rows], -1, h)
        for i, p in enumerate(ps):
            scatter(acc, go[i * h:(i + 1) * h], offs[p, 0], offs[p, 1], h)
    emit(acc, gl, gr)


def k_back_first(offs, g_in, probe, phase, tr, tl, gl, gr, acc):
    h, tab = phase.shape[1], tab_of(tr, tl)
    acc[...] = jnp.zeros_like(acc)
    for ps in groups(offs.shape[0]):
        n, rows = len(ps), rows_of(ps, h)
        g = propagate(g_in[rows], tab, phase, -1.0, h, n)
        go = times(g, tiled_probe(probe, n), -1, h)
        for i, p in enumerate(ps):
            scatter(acc, go[i * h:(i + 1) * h], offs[p, 0], offs[p, 1], h)
    emit(acc, gl, gr)


def on_device(object_field, probe, propagator, measured, offsets):
    slices, tile_r, tile_c = object_field.shape[1:]
    h, pos = probe.shape[1], offsets.shape[2]
    offs = offsets.reshape(pos, 2)
    target = measured.reshape(pos, h, h)
    phase = jnp.stack([jnp.cos(propagator), jnp.sin(propagator)])
    tr, tl = (jnp.asarray(t) for t in tables(h))

    wave = jax.ShapeDtypeStruct((pos * h, 2 * h), F32)
    ext = pltpu.VMEM((2, tile_r + h, tile_c + h), F32)
    grad = [jax.ShapeDtypeStruct((2, tile_r + h, tile_c), F32), jax.ShapeDtypeStruct((2, tile_r + h, h), F32)]
    flops = 8 * 2 * 2 * 2 * 3 * pos * h * (2 * h) ** 2
    cost = pl.CostEstimate(flops=flops, bytes_accessed=6_000_000, transcendentals=0)

    def call(body, outs, scratch, *args):
        vmem = pl.BlockSpec(memory_space=pltpu.VMEM)
        return pl.pallas_call(
            body,
            out_shape=outs,
            in_specs=[pl.BlockSpec(memory_space=pltpu.SMEM)] + [vmem] * len(args),
            out_specs=[vmem] * len(outs),
            scratch_shapes=scratch,
            cost_estimate=cost,
            compiler_params=pltpu.CompilerParams(vmem_limit_bytes=40 * 1024 * 1024),
        )(offs, *args)

    first, rest = object_field[:, 0], object_field[:, 1:].reshape(2 * slices - 2, tile_r, tile_c)
    tall_first = jnp.concatenate([first, passed_along(first[:, :h], "row", -1)], 1)
    tall_rest = jnp.concatenate([rest, passed_along(rest[:, :h], "row", -1)], 1)
    right_first = passed_along(tall_first[:, :, :h], "col", -1)
    right_rest = passed_along(tall_rest[:, :, :h], "col", -1)

    def layers(one, others):
        others = others.reshape(2, slices - 1, *others.shape[1:])
        return [one] + [others[:, s] for s in range(slices - 1)]

    tall, right = layers(after(tall_first, tall_rest), tall_rest), layers(right_first, right_rest)

    result = [None] * slices
    for step in range(ITERS):
        last = step + 1 == ITERS
        waves, objects = [None], [None]
        (w,) = call(k_first, [wave], [ext], tall[0], right[0], probe, phase, tr, tl)
        waves.append(w)
        for s in range(1, slices - 1):
            w, o = call(k_second, [wave, wave], [ext], tall[s], right[s], waves[s], phase, tr, tl)
            waves.append(w)
            objects.append(o)
        s = slices - 1
        totals = [None] * slices

        def widened(gl, gr):
            return gl.at[:, :, :h].add(passed_along(gr, "col", 1))

        gl, gr, g = call(k_last, grad + [wave], [ext, ext], tall[s], right[s], waves[s], target, tr, tl)
        totals[s] = widened(gl, gr)
        for s in range(slices - 2, -1, -1):
            if s + 2 < slices:
                g = after(g, totals[s + 2])
            if s:
                gl, gr, g = call(k_back, grad + [wave], [ext], g, waves[s], objects[s], phase, tr, tl)
            else:
                gl, gr = call(k_back_first, grad, [ext], g, probe, phase, tr, tl)
            totals[s] = widened(gl, gr)
        order = list(range(slices - 1, -1, -1))
        if not last:
            order = order[:1] + order[-1:] + order[1:-1]
        earlier = ()
        for s in order:
            total = after(totals[s], *earlier)
            above = passed_along(total[:, tile_r:], "row", 1)
            earlier = (above,)
            if last:
                result[s] = tall[s][:, :tile_r] - STEP * total[:, :tile_r].at[:, :h].add(above)
            else:
                below = passed_along(total[:, :h], "row", -1)
                earlier = (above, below)
                total = total.at[:, :h].add(above).at[:, tile_r:].add(below)
                tall[s] = tall[s] - STEP * total
                right[s] = passed_along(tall[s][:, :, :h], "col", -1)
    return jnp.stack(result, 1)


def solution(mesh):
    return jax.shard_map(
        on_device,
        mesh=mesh,
        in_specs=(
            P(None, None, "row", "col"),
            P(),
            P(),
            P("row", "col", None, None, None),
            P("row", "col", None, None),
        ),
        out_specs=P(None, None, "row", "col"),
        check_vma=False,
    )
```

```python
import jax
import jax.numpy as jnp
import numpy as np
from jax import lax
from jax.experimental import pallas as pl
from jax.experimental.pallas import tpu as pltpu
from jax.sharding import PartitionSpec as P

ITERS = 2
STEP = 0.05
SUB = 8
GROUP = 6
F32, BF16 = jnp.float32, jnp.bfloat16


def passed_along(block, axis, distance):
    n = lax.axis_size(axis)
    return lax.ppermute(block, axis, [((i - distance) % n, i) for i in range(n)])


def tables(h):
    k = np.arange(h)
    angle = (k[:, None] * k[None, :] % h) * (-2.0 * np.pi / h)
    c, s = np.cos(angle) / np.sqrt(h), np.sin(angle) / np.sqrt(h)

    def halves(m):
        m = m.astype(np.float32)
        high = m.astype(jnp.bfloat16)
        return high, (m - high.astype(np.float32)).astype(jnp.bfloat16)

    ah, al = halves(np.block([[c, s], [-s, c]]))
    bh, bl = halves(np.block([[c, -s], [s, c]]))
    return np.stack([ah, bh]), np.stack([al, bl])


def split(x):
    high = x.astype(BF16)
    return high, (x - high.astype(F32)).astype(BF16)


def mul_right(x, table):
    high, low = split(x)
    return jnp.dot(jnp.concatenate([high, low, high], 1), table, preferred_element_type=F32)


def mul_left(x, table):
    high, low = split(x)
    return jnp.dot(table, jnp.concatenate([high, low, high], 0), preferred_element_type=F32)


def to_left(x, h, n):
    return jnp.concatenate(
        [jnp.concatenate([x[p * h:(p + 1) * h, k * h:(k + 1) * h] for p in range(n)], 1) for k in range(2)], 0)


def to_right(x, h, n):
    return jnp.concatenate(
        [jnp.concatenate([x[k * h:(k + 1) * h, p * h:(p + 1) * h] for k in range(2)], 1) for p in range(n)], 0)


def dft(x, tab, h, n):
    return mul_left(to_left(mul_right(x, tab[0][0]), h, n), tab[1][0])


def idft(x, tab, h, n):
    return mul_right(to_right(mul_left(x, tab[1][1]), h, n), tab[0][1])


def propagate(x, tab, phase, sign, h, n):
    y = dft(x, tab, h, n)
    cr, ci = phase[0], phase[1] * sign
    cr, ci = (jnp.concatenate([v] * n, 1) for v in (cr, ci))
    a, b = y[:h], y[h:]
    return idft(jnp.concatenate([a * cr - b * ci, a * ci + b * cr], 0), tab, h, n)


def times(x, o, sign, h):
    a, b, c, d = x[:, :h], x[:, h:], o[:, :h], o[:, h:]
    if sign < 0:
        return jnp.concatenate([a * c + b * d, b * c - a * d], 1)
    return jnp.concatenate([a * c - b * d, a * d + b * c], 1)


def gather(ext, r, c, h):
    lane = lax.broadcasted_iota(jnp.int32, (h + SUB, h), 1)
    sub = lax.broadcasted_iota(jnp.int32, (h // SUB, SUB, h), 1)
    q, m, t = c // h, c % h, r % SUB
    parts = []
    for k in range(2):
        lines = ext[k, pl.ds(pl.multiple_of(r - t, SUB), h + SUB), pl.ds(pl.multiple_of(q * h, h), 2 * h)]
        mixed = jnp.where(lane >= m, lines[:, :h], lines[:, h:])
        mixed = pltpu.roll(mixed, (h - m) % h, 1).reshape(h // SUB + 1, SUB, h)
        mixed = jnp.where(sub >= t, mixed[:-1], mixed[1:])
        parts.append(pltpu.roll(mixed, (SUB - t) % SUB, 1).reshape(h, h))
    return jnp.concatenate(parts, 1)


def scatter(acc, g, r, c, h):
    lane = lax.broadcasted_iota(jnp.int32, (h + SUB, h), 1)
    sub = lax.broadcasted_iota(jnp.int32, (h // SUB + 1, SUB, h), 1)
    q, m, t = c // h, c % h, r % SUB
    empty = jnp.zeros((1, SUB, h), F32)
    for k in range(2):
        rolled = pltpu.roll(g[:, k * h:(k + 1) * h].reshape(h // SUB, SUB, h), t, 1)
        rolled = jnp.where(sub >= t, jnp.concatenate([rolled, empty], 0), jnp.concatenate([empty, rolled], 0))
        rolled = pltpu.roll(rolled.reshape(h + SUB, h), m, 1)
        keep = lane >= m
        pair = jnp.concatenate([jnp.where(keep, rolled, 0.0), jnp.where(keep, 0.0, rolled)], 1)
        at = (k, pl.ds(pl.multiple_of(r - t, SUB), h + SUB), pl.ds(pl.multiple_of(q * h, h), 2 * h))
        acc[at] = acc[at] + pair


def groups(n):
    size = GROUP if n % GROUP == 0 else 1
    return [list(range(i, i + size)) for i in range(0, n, size)]


def fill(ext, tall, right):
    w = tall.shape[2]
    ext[:, :, :w] = tall[...]
    ext[:, :, w:] = right[...]


def read_windows(ext, offs, ps, h):
    return jnp.concatenate([gather(ext, offs[p, 0], offs[p, 1], h) for p in ps], 0)


def tiled_probe(probe, n):
    one = jnp.concatenate([probe[0], probe[1]], 1)
    return jnp.concatenate([one] * n, 0)


def tab_of(tr, tl):
    pairs = [(tr[i], tl[i]) for i in range(2)]
    return ([jnp.concatenate([x, x, y], 0) for x, y in pairs], [jnp.concatenate([x, x, y], 1) for x, y in pairs[::-1]])


def rows_of(ps, h):
    return slice(ps[0] * h, (ps[-1] + 1) * h)


def k_first(offs, tall, right, probe, phase, tr, tl, w_out, ext):
    h, tab = probe.shape[1], tab_of(tr, tl)
    fill(ext, tall, right)
    for ps in groups(offs.shape[0]):
        n = len(ps)
        x = times(tiled_probe(probe, n), read_windows(ext, offs, ps, h), 1, h)
        w_out[rows_of(ps, h)] = propagate(x, tab, phase, 1.0, h, n)


def k_second(offs, tall, right, w_in, phase, tr, tl, w_out, o_out, ext):
    h, tab = phase.shape[1], tab_of(tr, tl)
    fill(ext, tall, right)
    for ps in groups(offs.shape[0]):
        n, rows = len(ps), rows_of(ps, h)
        o = read_windows(ext, offs, ps, h)
        o_out[rows] = o
        w_out[rows] = propagate(times(w_in[rows], o, 1, h), tab, phase, 1.0, h, n)


def emit(acc, gl, gr):
    w = gl.shape[2]
    gl[...] = acc[:, :, :w]
    gr[...] = acc[:, :, w:]


def k_last(offs, tall, right, w_in, measured, tr, tl, gl, gr, g_out, ext, acc):
    h, tab = measured.shape[1], tab_of(tr, tl)
    fill(ext, tall, right)
    acc[...] = jnp.zeros_like(acc)
    for ps in groups(offs.shape[0]):
        n, rows = len(ps), rows_of(ps, h)
        o = read_windows(ext, offs, ps, h)
        w = w_in[rows]
        far = dft(times(w, o, 1, h), tab, h, n)
        a, b = far[:h], far[h:]
        target = jnp.concatenate([measured[p] for p in ps], 1)
        f = 4.0 * (a * a + b * b - target)
        g = idft(jnp.concatenate([a * f, b * f], 0), tab, h, n)
        go = times(g, w, -1, h)
        g_out[rows] = times(g, o, -1, h)
        for i, p in enumerate(ps):
            scatter(acc, go[i * h:(i + 1) * h], offs[p, 0], offs[p, 1], h)
    emit(acc, gl, gr)


def k_back(offs, g_in, w_in, o_in, phase, tr, tl, gl, gr, g_out, acc):
    h, tab = phase.shape[1], tab_of(tr, tl)
    acc[...] = jnp.zeros_like(acc)
    for ps in groups(offs.shape[0]):
        n, rows = len(ps), rows_of(ps, h)
        g = propagate(g_in[rows], tab, phase, -1.0, h, n)
        go = times(g, w_in[rows], -1, h)
        g_out[rows] = times(g, o_in[rows], -1, h)
        for i, p in enumerate(ps):
            scatter(acc, go[i * h:(i + 1) * h], offs[p, 0], offs[p, 1], h)
    emit(acc, gl, gr)


def k_back_first(offs, g_in, probe, phase, tr, tl, gl, gr, acc):
    h, tab = phase.shape[1], tab_of(tr, tl)
    acc[...] = jnp.zeros_like(acc)
    for ps in groups(offs.shape[0]):
        n, rows = len(ps), rows_of(ps, h)
        g = propagate(g_in[rows], tab, phase, -1.0, h, n)
        go = times(g, tiled_probe(probe, n), -1, h)
        for i, p in enumerate(ps):
            scatter(acc, go[i * h:(i + 1) * h], offs[p, 0], offs[p, 1], h)
    emit(acc, gl, gr)


def on_device(object_field, probe, propagator, measured, offsets):
    slices, tile_r, tile_c = object_field.shape[1:]
    h, pos = probe.shape[1], offsets.shape[2]
    offs = offsets.reshape(pos, 2)
    target = measured.reshape(pos, h, h)
    phase = jnp.stack([jnp.cos(propagator), jnp.sin(propagator)])
    tr, tl = (jnp.asarray(t) for t in tables(h))

    wave = jax.ShapeDtypeStruct((pos * h, 2 * h), F32)
    ext = pltpu.VMEM((2, tile_r + h, tile_c + h), F32)
    grad = [jax.ShapeDtypeStruct((2, tile_r + h, tile_c), F32), jax.ShapeDtypeStruct((2, tile_r + h, h), F32)]
    flops = 2 * 2 * 2 * 3 * pos * h * (2 * h) ** 2
    cost = pl.CostEstimate(flops=flops, bytes_accessed=6_000_000, transcendentals=0)

    def call(body, outs, scratch, *args):
        vmem = pl.BlockSpec(memory_space=pltpu.VMEM)
        return pl.pallas_call(
            body,
            out_shape=outs,
            in_specs=[pl.BlockSpec(memory_space=pltpu.SMEM)] + [vmem] * len(args),
            out_specs=[vmem] * len(outs),
            scratch_shapes=scratch,
            cost_estimate=cost,
            compiler_params=pltpu.CompilerParams(vmem_limit_bytes=40 * 1024 * 1024),
        )(offs, *args)

    tall, right = [], []
    for s in range(slices):
        own = object_field[:, s]
        tall.append(jnp.concatenate([own, passed_along(own[:, :h], "row", -1)], 1))
    for s in range(slices):
        right.append(passed_along(tall[s][:, :, :h], "col", -1))

    result = [None] * slices
    for step in range(ITERS):
        waves, objects = [None], [None]
        (w,) = call(k_first, [wave], [ext], tall[0], right[0], probe, phase, tr, tl)
        waves.append(w)
        for s in range(1, slices - 1):
            w, o = call(k_second, [wave, wave], [ext], tall[s], right[s], waves[s], phase, tr, tl)
            waves.append(w)
            objects.append(o)
        s = slices - 1
        grads = [None] * slices
        *grads[s], g = call(k_last, grad + [wave], [ext, ext], tall[s], right[s], waves[s], target, tr, tl)
        for s in range(slices - 2, 0, -1):
            *grads[s], g = call(k_back, grad + [wave], [ext], g, waves[s], objects[s], phase, tr, tl)
        grads[0] = call(k_back_first, grad, [ext], g, probe, phase, tr, tl)
        last = step + 1 == ITERS
        for s in range(slices - 1, -1, -1):
            gl, gr = grads[s]
            total = gl.at[:, :, :h].add(passed_along(gr, "col", 1))
            above = passed_along(total[:, tile_r:], "row", 1)
            if last:
                result[s] = tall[s][:, :tile_r] - STEP * total[:, :tile_r].at[:, :h].add(above)
            else:
                below = passed_along(total[:, :h], "row", -1)
                total = total.at[:, :h].add(above).at[:, tile_r:].add(below)
                tall[s] = tall[s] - STEP * total
                right[s] = passed_along(tall[s][:, :, :h], "col", -1)
    return jnp.stack(result, 1)


def solution(mesh):
    return jax.shard_map(
        on_device,
        mesh=mesh,
        in_specs=(
            P(None, None, "row", "col"),
            P(),
            P(),
            P("row", "col", None, None, None),
            P("row", "col", None, None),
        ),
        out_specs=P(None, None, "row", "col"),
        check_vma=False,
    )
```
